256 devices in a mesh: gx: 4 (over y), yz: 64 (over z, x, core).
Axes of the slice: x: 4, y: 4, z: 8, core: 2. Of those that a mesh axis runs over, the one named last changes fastest.
Arguments:
- potential: float32 [32, 512, 2048], P('gx', 'yz'), may hold values from -96 to 96
- gal_cells: int32 [4, 64, 64, 128], P('gx', 'yz'), may hold values from 0 to 63
- gal_z: int32 [4, 64, 64, 128], P('gx', 'yz'), may hold values from 0 to 2047
- gal_bins: int32 [4, 64, 64, 128], P('gx', 'yz'), may hold values from 0 to 7
- gal_counts: int32 [4, 64, 64], P('gx', 'yz'), may hold values from 1 to 128, as said below
Outputs:
- tidal: float32 [6, 4, 64, 8192], P(None, 'gx', 'yz')
The draws below stay inside these ranges and needn't reach their ends.
Inputs may be any that keep to these rules, and one draw needn't show every extreme that they name: For each band g, one tile d receives 128 live slots from every home device; the live slots are the first gal_counts ones.
All inputs are finite; a program needn't handle non-finite values.
Results may differ from the reference program's by a relative error of at most 0.00002.
Values sent between devices are 32-bit elements; how exact they have to be, the bound alone decides.
A program may use at most 192 MiB of HBM per device.

```python
import jax
import jax.numpy as jnp
from jax import lax

CX = 8
CY = 8
CZ = 2048
CAP = 128
HALO = 6
BINS = 8
NX = 32
NY = 512
N_GX = 4
N_YZ = 64


def draw_gal_counts(key, part):
    lowest = max(1, CAP // 4)
    counts = jax.random.randint(jax.random.fold_in(key, 11), (N_GX, N_YZ, N_YZ), lowest, CAP + 1)
    hot_tile = jax.random.randint(jax.random.fold_in(key, 12), (N_GX, 1, 1), 0, N_YZ)
    columns = lax.broadcasted_iota(jnp.int32, (N_GX, N_YZ, N_YZ), 2)
    return jnp.where(columns == hot_tile, CAP, counts).astype(jnp.int32)


def plant(drawn, key, least, high):
    shape = drawn.shape
    index_at = [jax.random.randint(jax.random.fold_in(key, axis), (), 0, shape[axis]) for axis in range(len(shape))]
    drawn = drawn.at[tuple(index_at)].set(least)
    longest = shape.index(max(shape))
    index_at[longest] = (index_at[longest] + 1) % shape[longest]
    return drawn.at[tuple(index_at)].set(high)


def steps_of(own_key, extent, split, smallest, top_value):
    gain = 1.0
    for axis_at, blocks in split:
        heights = jax.random.uniform(jax.random.fold_in(jax.random.fold_in(own_key, 6), axis_at), (blocks,), jnp.float32, smallest / len(split), top_value / len(split))
        gain = gain * jnp.repeat(jnp.exp(heights), extent[axis_at] // blocks).reshape((-1,) + (1,) * (len(extent) - 1 - axis_at))
    return gain


def normal_values(rng, dims, width, most, cuts=(), held_as=jnp.bfloat16):
    drawn = jax.random.normal(rng, dims, jnp.float32) * width
    if len(cuts) > 0:
        drawn = steps_of(rng, dims, cuts, -0.22, 0.18) * drawn
    return jnp.clip(drawn, min=-most, max=most).astype(held_as)


def setup_inputs(seed: int = 0) -> dict:
    keys = jax.random.split(jax.random.key(seed), 6)
    potential = normal_values(keys[0], (NX, NY, CZ), 16.0, 96.0, ((0, 4), (1, 64)), jnp.float32)
    gal_cells = plant(jax.random.randint(keys[1], (N_GX, N_YZ, N_YZ, CAP), 0, CX * CY), jax.random.fold_in(keys[1], 1), 0, (CX * CY) - 1).astype(jnp.int32)
    gal_z = plant(jax.random.randint(keys[2], (N_GX, N_YZ, N_YZ, CAP), 0, CZ), jax.random.fold_in(keys[2], 1), 0, CZ - 1).astype(jnp.int32)
    gal_bins = plant(jax.random.randint(keys[3], (N_GX, N_YZ, N_YZ, CAP), 0, BINS), jax.random.fold_in(keys[3], 1), 0, BINS - 1).astype(jnp.int32)
    gal_counts = draw_gal_counts(jax.random.fold_in(keys[5], 71), 0)
    return {"potential": potential, "gal_cells": gal_cells, "gal_z": gal_z, "gal_bins": gal_bins, "gal_counts": gal_counts}


def kernels():
    offsets = jnp.arange(-HALO, HALO + 1).astype(jnp.float32)
    sigma_cells = HALO / 3.0
    smooth_w = jnp.exp(-offsets * offsets / (2.0 * sigma_cells * sigma_cells))
    smooth_w = smooth_w / jnp.sum(smooth_w)
    first_w = offsets / (sigma_cells * sigma_cells) * smooth_w
    second_w = (offsets * offsets / sigma_cells ** 4 - 1.0 / (sigma_cells * sigma_cells)) * smooth_w
    return smooth_w, first_w, second_w


def sweep_axis(padded, weights, axis):
    length = padded.shape[axis] - 2 * HALO
    summed = weights[0] * lax.slice_in_dim(padded, 0, length, axis=axis)
    for k in range(1, 2 * HALO + 1):
        summed = summed + weights[k] * lax.slice_in_dim(padded, k, k + length, axis=axis)
    return summed


def plan_list(along_x, weights):
    x_smooth, x_first, x_second = along_x
    smooth_w, first_w, second_w = weights
    return [(x_second, smooth_w, smooth_w), (x_smooth, second_w, smooth_w), (x_smooth, smooth_w, second_w),
            (x_first, first_w, smooth_w), (x_first, smooth_w, first_w), (x_smooth, first_w, first_w)]


def one_component(field, y_w, z_w):
    in_y = sweep_axis(field, y_w, 1)
    wrapped = jnp.concatenate([in_y[:, :, -HALO:], in_y, in_y[:, :, :HALO]], axis=2)
    return sweep_axis(wrapped, z_w, 2)


def reference(potential, gal_cells, gal_z, gal_bins, gal_counts):
    weights = kernels()
    padded = jnp.pad(potential, ((HALO, HALO), (HALO, HALO), (0, 0)))
    along_x = [sweep_axis(padded, w, 0) for w in weights]
    scale = (HALO / 3.0) ** 2
    shape = gal_cells.shape
    band = lax.broadcasted_iota(jnp.int32, shape, 0)
    tile = lax.broadcasted_iota(jnp.int32, shape, 2)
    slot = lax.broadcasted_iota(jnp.int32, shape, 3)
    plane = gal_cells // CY
    row_in = gal_cells % CY
    z_index = gal_z
    x_global = band * CX + plane
    y_global = tile * CY + row_in
    z_next = (z_index + 1) % CZ
    weight = (gal_bins.astype(jnp.float32) + 0.5) / BINS
    live = slot < gal_counts[:, :, :, None]
    results = []
    for field, y_w, z_w in plan_list(along_x, weights):
        comp = one_component(field, y_w, z_w)
        here_value = comp[x_global, y_global, z_index]
        next_value = comp[x_global, y_global, z_next]
        value = ((1.0 - weight) * here_value + weight * next_value) * scale
        results.append(jnp.where(live, value, jnp.float32(0.0)))
    tidal = jnp.stack(results)
    return tidal.reshape(6, N_GX, N_YZ, N_YZ * CAP)
```

```python
import functools

import jax
import jax.numpy as jnp
import ml_dtypes
import numpy as np
from jax import lax
from jax.experimental import pallas as pl
from jax.experimental.pallas import tpu as pltpu
from jax.sharding import PartitionSpec as P

HALO = 6
BINS = 8
SIGMA = HALO / 3.0
OFF = 32
MESH = pl.DeviceIdType.MESH
CHUNKS = 4
KROWS = 416
KALL = 2560
PARTS = (0, 1, 2, 0, 1, 0)
WEIGHT_PARTS = (0, 0, 0, 1, 1, 2)
ORDER = (0, 1, 5, 2, 3, 4)
GROUPS = ((0, 192, 0), (192, 320, 1), (320, 384, 2))


def filters():
    k = np.arange(-HALO, HALO + 1).astype(np.float64)
    w0 = np.exp(-k * k / (2.0 * SIGMA * SIGMA))
    w0 = w0 / w0.sum()
    return w0, k / SIGMA**2 * w0, (k * k / SIGMA**4 - 1.0 / SIGMA**2) * w0


def split3(a):
    parts = []
    for _ in range(3):
        p = a.astype(ml_dtypes.bfloat16)
        parts.append(p)
        a = a - p.astype(np.float64)
    return parts


def plane_weights():
    w = filters()
    rows = [(x, y) for x in range(8) for y in range(8)]
    rows += [(x, y) for x in range(-6, 0) for y in range(8)]
    rows += [(x, y) for x in range(8, 14) for y in range(8)]
    rows += [(x, y) for x in range(8) for y in range(-6, 0)]
    rows += [(x, y) for x in range(8) for y in range(8, 14)]
    outer = list(range(-6, 0)) + list(range(8, 14))
    for ys in (range(-6, 0), range(8, 14)):
        rows += [(x, y) for x in outer for y in ys] + [None] * 8
    pairs = ((2, 0), (0, 2), (1, 1), (1, 0), (0, 1), (0, 0))
    a = np.zeros((6, 8, 8, KROWS))
    for k, at in enumerate(rows):
        if at is None:
            continue
        for xo in range(8):
            dx = at[0] - xo + HALO
            for yo in range(8):
                dy = at[1] - yo + HALO
                if 0 <= dx <= 2 * HALO and 0 <= dy <= 2 * HALO:
                    for c, (fx, fy) in enumerate(pairs):
                        a[c, xo, yo, k] = w[fx][dx] * w[fy][dy]
    parts = split3(a.reshape(384, KROWS))
    out = np.zeros((384, KALL), ml_dtypes.bfloat16)
    for i, p in enumerate(WEIGHT_PARTS):
        out[:, i * KROWS : (i + 1) * KROWS] = parts[p]
    return out


def band_weights():
    w = filters()
    out = np.zeros((3, 6 * 256, 256), ml_dtypes.bfloat16)
    for f in range(3):
        band = np.zeros((256, 256))
        for half in range(2):
            for lane in range(128):
                for tap in range(2 * HALO + 1):
                    band[half * 64 + OFF + lane + tap - HALO, half * 128 + lane] = w[f][tap]
        parts = split3(band)
        for i, p in enumerate(WEIGHT_PARTS):
            out[f, i * 256 : (i + 1) * 256] = parts[p]
    return out


def kernel(
    n_gx, n_yz, pot, cells, zeds, bins, plane_hbm, band_hbm, out,
    msg, slots, xb, xa, up, down, cup, cdown, yb, ya, cb, ca,
    plane_w, band_w, pall, gpart, tab, wrow, addr_v, addr_s, served, returned,
    local_sem, slot_send, slot_recv, x_send, x_recv, y_send, y_recv, c_send, c_recv, ret_send, ret_recv,
):
    g = lax.axis_index("gx")
    t = lax.axis_index("yz")
    zc = pot.shape[2] // CHUNKS
    g_up, g_down = lax.rem(g + 1, n_gx), lax.rem(g + n_gx - 1, n_gx)
    t_up, t_down = lax.rem(t + 1, n_yz), lax.rem(t + n_yz - 1, n_yz)

    barrier = pltpu.get_barrier_semaphore()

    @pl.loop(1, n_yz)
    def _(i):
        pl.semaphore_signal(barrier, inc=1, device_id=(g, lax.rem(t + i, n_yz)), device_id_type=MESH)

    for other in (g_up, g_down):
        pl.semaphore_signal(barrier, inc=1, device_id=(other, t), device_id_type=MESH)

    plane_in = pltpu.make_async_copy(plane_hbm, plane_w, local_sem.at[0])
    band_in = pltpu.make_async_copy(band_hbm, band_w, local_sem.at[1])
    plane_in.start()
    band_in.start()
    for i, ref in enumerate((cells, zeds, bins)):
        msg[:, i, :] = ref[...]
    for p in range(8):
        up[6 * p : 6 * p + 6, :] = pot[p, 2:8, :]
        down[6 * p : 6 * p + 6, :] = pot[p, 0:6, :]
    pl.semaphore_wait(barrier, n_yz + 1)

    def remote(src, dst, send, recv, to):
        return pltpu.make_async_remote_copy(
            src_ref=src, dst_ref=dst, send_sem=send, recv_sem=recv, device_id=to, device_id_type=MESH
        )

    x_copies, y_copies, c_copies = [], [], []
    for c in range(CHUNKS):
        zs = pl.ds(c * zc, zc)
        x_copies.append((
            remote(pot.at[pl.ds(2, 6), :, zs], xb.at[:, :, zs], x_send.at[0, c], x_recv.at[0, c], (g_up, t)),
            remote(pot.at[pl.ds(0, 6), :, zs], xa.at[:, :, zs], x_send.at[1, c], x_recv.at[1, c], (g_down, t)),
        ))
        y_copies.append((
            remote(up.at[:, zs], yb.at[:, zs], y_send.at[0, c], y_recv.at[0, c], (g, t_up)),
            remote(down.at[:, zs], ya.at[:, zs], y_send.at[1, c], y_recv.at[1, c], (g, t_down)),
        ))
        c_copies.append((
            remote(cup.at[:, zs], cb.at[:, zs], c_send.at[0, c], c_recv.at[0, c], (g, t_up)),
            remote(cdown.at[:, zs], ca.at[:, zs], c_send.at[1, c], c_recv.at[1, c], (g, t_down)),
        ))
    for copy in x_copies[0] + y_copies[0]:
        copy.start()

    @pl.loop(1, n_yz)
    def _(i):
        to = lax.rem(t + i, n_yz)
        remote(msg.at[to], slots.at[t], slot_send, slot_recv, (g, to)).start()

    own = pltpu.make_async_copy(msg.at[t], slots.at[t], slot_recv)
    own.start()
    for c in range(1, CHUNKS):
        for copy in x_copies[c] + y_copies[c]:
            copy.start()

    pltpu.make_async_copy(msg, slots, slot_recv).wait()
    zr = jnp.bitwise_and(slots[:, 1, :] - OFF, 2047)
    addr_v[...] = slots[:, 0, :] * 32 + jnp.right_shift(zr, 6)
    to_scalar = pltpu.make_async_copy(addr_v, addr_s, local_sem.at[2])
    to_scalar.start()
    zl = jnp.bitwise_and(zr, 63).astype(jnp.float32)
    weight = (slots[:, 2, :].astype(jnp.float32) + 0.5) / BINS
    lane = lax.broadcasted_iota(jnp.int32, (128, 128), 1).astype(jnp.float32)
    columns = jnp.transpose(jnp.concatenate([zl, weight], axis=0))

    def interpolation_rows(homes):
        scale = SIGMA * SIGMA
        for h in homes:
            z_at = columns[:, h : h + 1]
            w_at = columns[:, 64 + h : 65 + h] * scale
            wrow[h] = jnp.where(lane == z_at, scale - w_at, jnp.where(lane == z_at + 1.0, w_at, 0.0))

    def corners(c):
        zs = pl.ds(c * zc, zc)
        for copy in x_copies[c]:
            copy.wait_recv()
        for side, ref, live in ((0, xb, g > 0), (1, xa, g < n_gx - 1)):
            @pl.when(jnp.logical_not(live))
            def _():
                ref[:, :, zs] = jnp.zeros((6, 8, zc), jnp.float32)

            for q in range(6):
                at = 36 * side + 6 * q
                cup[at : at + 6, zs] = ref[q, 2:8, zs]
                cdown[at : at + 6, zs] = ref[q, 0:6, zs]
        for copy in c_copies[c]:
            copy.start()

    step = 64 // CHUNKS
    for c in range(CHUNKS):
        corners(c)
        interpolation_rows(range(c * step, (c + 1) * step))

    pall[6 * KROWS :, :] = jnp.zeros((KALL - 6 * KROWS, zc), jnp.bfloat16)

    def place(at, x):
        rows = x.shape[0]
        p1 = x.astype(jnp.bfloat16)
        r = x - p1.astype(jnp.float32)
        p2 = r.astype(jnp.bfloat16)
        p3 = (r - p2.astype(jnp.float32)).astype(jnp.bfloat16)
        parts = (p1, p2, p3)
        for i, p in enumerate(PARTS):
            pall[i * KROWS + at : i * KROWS + at + rows, :] = parts[p]

    plane_in.wait()
    band_in.wait()

    flat = tab.reshape(64 * 32 * 8, 128)

    def windows(lo, hi):
        for a, b, f in GROUPS:
            lhs = jnp.concatenate(
                [
                    jnp.concatenate([gpart[p, a:b, 128 * w : 128 * w + 256] for p in PARTS], axis=1)
                    for w in range(lo, hi)
                ],
                axis=0,
            )
            h = jnp.dot(lhs, band_w[f], preferred_element_type=jnp.float32)
            at = 0
            for w in range(lo, hi):
                for comp in range(a // 64, b // 64):
                    for ct in range(8):
                        for half in range(2):
                            v = h[at : at + 8, 128 * half : 128 * half + 128]
                            first = ((8 * ct) * 32 + 2 * w + half) * 8 + comp
                            flat[pl.ds(first, 8, stride=256), :] = v
                        at += 8

    for c in range(CHUNKS):
        zs = pl.ds(c * zc, zc)
        place(0, pot[:, :, zs].reshape(64, zc))
        place(64, xb[:, :, zs].reshape(48, zc))
        place(112, xa[:, :, zs].reshape(48, zc))
        for copy in y_copies[c] + c_copies[c]:
            copy.wait_recv()
        first, last = t > 0, t < n_yz - 1
        place(160, jnp.where(first, yb[:, zs], 0.0))
        place(208, jnp.where(last, ya[:, zs], 0.0))
        zero8 = jnp.zeros((8, zc), jnp.float32)
        place(256, jnp.concatenate([jnp.where(first, cb[:, zs], 0.0), zero8], axis=0))
        place(336, jnp.concatenate([jnp.where(last, ca[:, zs], 0.0), zero8], axis=0))
        field = jnp.dot(plane_w[...], pall[...], preferred_element_type=jnp.float32)
        g1 = field.astype(jnp.bfloat16)
        r = field - g1.astype(jnp.float32)
        g2 = r.astype(jnp.bfloat16)
        g3 = (r - g2.astype(jnp.float32)).astype(jnp.bfloat16)
        for p, part in enumerate((g1, g2, g3)):
            gpart[p, :, c * zc : (c + 1) * zc] = part
            if c == 0:
                gpart[p, :, 2048:2176] = part[:, 0:128]
        lo = 0 if c == 0 else 4 * c - 1
        hi = 4 * c + 3 if c < CHUNKS - 1 else 16
        windows(lo, hi)

    to_scalar.wait()
    lane8 = lax.broadcasted_iota(jnp.int32, (8, 128), 1)

    @pl.loop(0, n_yz // 4)
    def _(i):
        homes = [lax.rem(t + 1 + i * 4 + k, n_yz) for k in range(4)]
        for h in homes:
            acc = jnp.zeros((8, 128), jnp.float32)
            for j in range(128):
                row = addr_s[h, j]
                p = tab[row] * wrow[h, pl.ds(j, 1), :]
                acc = jnp.where(lane8 == j, jnp.sum(p, axis=1, keepdims=True), acc)
            served[h] = acc
        for h in homes:
            @pl.when(h != t)
            def _():
                remote(served.at[h], returned.at[t], ret_send, ret_recv, (g, h)).start()

            @pl.when(h == t)
            def _():
                pltpu.make_async_copy(served.at[h], returned.at[t], ret_recv).start()

    pltpu.make_async_copy(served, returned, ret_recv).wait()
    for a, at in enumerate(ORDER):
        out[a] = returned[:, at, :]
    pltpu.make_async_copy(served.at[pl.ds(0, n_yz - 1)], returned.at[pl.ds(0, n_yz - 1)], ret_send).wait()
    pltpu.make_async_copy(msg.at[pl.ds(0, n_yz - 1)], slots.at[pl.ds(0, n_yz - 1)], slot_send).wait()
    for c in range(CHUNKS):
        for copy in x_copies[c] + y_copies[c] + c_copies[c]:
            copy.wait_send()


def body(n_gx, n_yz, potential, gal_cells, gal_z, gal_bins, gal_counts):
    tiles, cap = gal_cells.shape[2], gal_cells.shape[3]
    cz = potential.shape[2]
    f32, bf16, i32 = jnp.float32, jnp.bfloat16, jnp.int32
    vmem = pl.BlockSpec(memory_space=pltpu.VMEM)
    hbm = pl.BlockSpec(memory_space=pl.ANY)
    dma = pltpu.SemaphoreType.DMA
    returned = pl.pallas_call(
        functools.partial(kernel, n_gx, n_yz),
        out_shape=jax.ShapeDtypeStruct((6, tiles, cap), f32),
        in_specs=[vmem] * 4 + [hbm] * 2,
        out_specs=vmem,
        scratch_shapes=[
            pltpu.VMEM((tiles, 4, cap), i32),
            pltpu.VMEM((tiles, 4, cap), i32),
            pltpu.VMEM((6, 8, cz), f32),
            pltpu.VMEM((6, 8, cz), f32),
            pltpu.VMEM((48, cz), f32),
            pltpu.VMEM((48, cz), f32),
            pltpu.VMEM((72, cz), f32),
            pltpu.VMEM((72, cz), f32),
            pltpu.VMEM((48, cz), f32),
            pltpu.VMEM((48, cz), f32),
            pltpu.VMEM((72, cz), f32),
            pltpu.VMEM((72, cz), f32),
            pltpu.VMEM((384, KALL), bf16),
            pltpu.VMEM((3, 1536, 256), bf16),
            pltpu.VMEM((KALL, cz // CHUNKS), bf16),
            pltpu.VMEM((3, 384, cz + 128), bf16),
            pltpu.VMEM((64 * 32, 8, 128), f32),
            pltpu.VMEM((tiles, cap, 128), f32),
            pltpu.VMEM((tiles, cap), i32),
            pltpu.SMEM((tiles, cap), i32),
            pltpu.VMEM((tiles, 8, cap), f32),
            pltpu.VMEM((tiles, 8, cap), f32),
            dma((3,)),
            dma,
            dma,
            dma((2, CHUNKS)),
            dma((2, CHUNKS)),
            dma((2, CHUNKS)),
            dma((2, CHUNKS)),
            dma((2, CHUNKS)),
            dma((2, CHUNKS)),
            dma,
            dma,
        ],
        compiler_params=pltpu.CompilerParams(
            collective_id=0, has_side_effects=True, vmem_limit_bytes=60 * 1024 * 1024
        ),
        name="tidal",
    )(
        potential,
        gal_cells.reshape(tiles, cap),
        gal_z.reshape(tiles, cap),
        gal_bins.reshape(tiles, cap),
        jnp.asarray(plane_weights()),
        jnp.asarray(band_weights()),
    )
    slot_index = lax.broadcasted_iota(jnp.int32, (tiles, cap), 1)
    live = slot_index < gal_counts.reshape(tiles, 1)
    tidal = jnp.where(live[None], returned, jnp.float32(0.0))
    return tidal.reshape(6, 1, 1, tiles * cap)


def solution(mesh):
    return jax.shard_map(
        functools.partial(body, mesh.shape["gx"], mesh.shape["yz"]),
        mesh=mesh,
        in_specs=(
            P("gx", "yz", None),
            P("gx", "yz", None, None),
            P("gx", "yz", None, None),
            P("gx", "yz", None, None),
            P("gx", "yz", None),
        ),
        out_specs=P(None, "gx", "yz", None),
        check_vma=False,
    )
```

```python
import functools

import jax
import jax.numpy as jnp
import ml_dtypes
import numpy as np
from jax import lax
from jax.experimental import pallas as pl
from jax.experimental.pallas import tpu as pltpu
from jax.sharding import PartitionSpec as P

HALO = 6
BINS = 8
SIGMA = HALO / 3.0
STEP = 116
MESH = pl.DeviceIdType.MESH
CHUNKS = 4
PLANE = 8
STRIDE = 1
WINDOWS = 19
FIRST = 160
SECOND = 256
KROWS = FIRST + SECOND
KFIRST, KSECOND = 1024, 6 * SECOND
PARTS = (0, 1, 2, 0, 1, 0)
WEIGHT_PARTS = (0, 0, 0, 1, 1, 2)
ORDER = (0, 1, 5, 2, 3, 4)
GROUPS = ((0, 192, 0), (192, 320, 1), (320, 384, 2))


def filters():
    k = np.arange(-HALO, HALO + 1).astype(np.float64)
    w0 = np.exp(-k * k / (2.0 * SIGMA * SIGMA))
    w0 = w0 / w0.sum()
    return w0, k / SIGMA**2 * w0, (k * k / SIGMA**4 - 1.0 / SIGMA**2) * w0


def split3(a):
    parts = []
    for _ in range(3):
        p = a.astype(ml_dtypes.bfloat16)
        parts.append(p)
        a = a - p.astype(np.float64)
    return parts


def plane_weights():
    w = filters()
    rows = [(x, y) for x in range(8) for y in range(8)]
    rows += [(x, y) for x in range(-6, 0) for y in range(8)]
    rows += [(x, y) for x in range(8, 14) for y in range(8)]
    rows += [(x, y) for x in range(8) for y in range(-6, 0)]
    rows += [(x, y) for x in range(8) for y in range(8, 14)]
    outer = list(range(-6, 0)) + list(range(8, 14))
    for ys in (range(-6, 0), range(8, 14)):
        rows += [(x, y) for x in outer for y in ys] + [None] * 8
    pairs = ((2, 0), (0, 2), (1, 1), (1, 0), (0, 1), (0, 0))
    a = np.zeros((6, 8, 8, KROWS))
    for k, at in enumerate(rows):
        if at is None:
            continue
        for xo in range(8):
            dx = at[0] - xo + HALO
            for yo in range(8):
                dy = at[1] - yo + HALO
                if 0 <= dx <= 2 * HALO and 0 <= dy <= 2 * HALO:
                    for c, (fx, fy) in enumerate(pairs):
                        a[c, xo, yo, k] = w[fx][dx] * w[fy][dy]
    parts = split3(a.reshape(384, KROWS))
    out = np.zeros((384, KFIRST + KSECOND), ml_dtypes.bfloat16)
    for i, p in enumerate(WEIGHT_PARTS):
        out[:, i * FIRST : (i + 1) * FIRST] = parts[p][:, :FIRST]
        at = KFIRST + i * SECOND
        out[:, at : at + SECOND] = parts[p][:, FIRST:]
    return out


def band_weights():
    w = filters()
    out = np.zeros((3, 6 * 256, 256), ml_dtypes.bfloat16)
    for f in range(3):
        band = np.zeros((256, 256))
        for half in range(2):
            for lane in range(128):
                for tap in range(2 * HALO + 1):
                    band[half * STEP + lane + tap, half * 128 + lane] = w[f][tap]
        parts = split3(band)
        for i, p in enumerate(WEIGHT_PARTS):
            out[f, i * 256 : (i + 1) * 256] = parts[p]
    return out


def kernel(
    n_gx, n_yz, pot_hbm, cells_hbm, zeds_hbm, bins_hbm, counts_hbm, plane_hbm, band_hbm, out,
    pot, cells, zeds, bins, counts, msg, slots, xb, xa, up, down, cup, cdown, yb, ya, cb, ca,
    plane_w, band_w, first_in, second_in, partial, tab, wrow, addr_v, addr_s, served, returned, live,
    local_sem, in_sem, ready, slot_send, slot_recv, x_send, x_recv, y_send, y_recv, c_send, c_recv, ret_send, ret_recv,
):
    g = lax.axis_index("gx")
    t = lax.axis_index("yz")
    zc = pot.shape[2] // CHUNKS
    g_up, g_down = lax.rem(g + 1, n_gx), lax.rem(g + n_gx - 1, n_gx)
    t_up, t_down = lax.rem(t + 1, n_yz), lax.rem(t + n_yz - 1, n_yz)

    barrier = pltpu.get_barrier_semaphore()

    z, q = t // PLANE, lax.rem(t, PLANE)
    lines = n_yz // PLANE
    in_plane = [(g, z * PLANE + lax.rem(q + i, PLANE)) for i in range(1, PLANE)]
    in_line = [(g, lax.rem(z + i, lines) * PLANE + q) for i in range(1, lines)]
    for to in [(g_up, t), (g_down, t)] + in_plane + in_line:
        pl.semaphore_signal(barrier, inc=1, device_id=to, device_id_type=MESH)

    @pl.when(q == PLANE - 1)
    def _():
        pl.semaphore_signal(barrier, inc=1, device_id=(g, t_up), device_id_type=MESH)

    @pl.when(q == 0)
    def _():
        pl.semaphore_signal(barrier, inc=1, device_id=(g, t_down), device_id_type=MESH)

    loads = [
        pltpu.make_async_copy(src, dst, in_sem.at[i])
        for i, (src, dst) in enumerate(
            ((pot_hbm, pot), (cells_hbm, cells), (zeds_hbm, zeds), (bins_hbm, bins), (counts_hbm, counts))
        )
    ]
    for load in loads:
        load.start()
    plane_in = pltpu.make_async_copy(plane_hbm, plane_w, local_sem.at[0])
    band_in = pltpu.make_async_copy(band_hbm, band_w, local_sem.at[1])
    plane_in.start()
    band_in.start()
    for load in loads:
        load.wait()
    for i, ref in enumerate((cells, zeds, bins)):
        msg[:, i, :] = ref[...]
    for p in range(8):
        up[6 * p : 6 * p + 6, :] = pot[p, 2:8, :]
        down[6 * p : 6 * p + 6, :] = pot[p, 0:6, :]
    edge = jnp.logical_or(q == PLANE - 1, q == 0)

    @pl.when(edge)
    def _():
        pl.semaphore_wait(barrier, PLANE + lines + 1)

    @pl.when(jnp.logical_not(edge))
    def _():
        pl.semaphore_wait(barrier, PLANE + lines)

    def remote(src, dst, send, recv, to):
        return pltpu.make_async_remote_copy(
            src_ref=src, dst_ref=dst, send_sem=send, recv_sem=recv, device_id=to, device_id_type=MESH
        )

    x_copies, y_copies, c_copies = [], [], []
    for c in range(CHUNKS):
        zs = pl.ds(c * zc, zc)
        x_copies.append((
            remote(pot.at[pl.ds(2, 6), :, zs], xb.at[:, :, zs], x_send.at[0, c], x_recv.at[0, c], (g_up, t)),
            remote(pot.at[pl.ds(0, 6), :, zs], xa.at[:, :, zs], x_send.at[1, c], x_recv.at[1, c], (g_down, t)),
        ))
        y_copies.append((
            remote(up.at[:, zs], yb.at[:, zs], y_send.at[0, c], y_recv.at[0, c], (g, t_up)),
            remote(down.at[:, zs], ya.at[:, zs], y_send.at[1, c], y_recv.at[1, c], (g, t_down)),
        ))
        c_copies.append((
            remote(cup.at[:, zs], cb.at[:, zs], c_send.at[0, c], c_recv.at[0, c], (g, t_up)),
            remote(cdown.at[:, zs], ca.at[:, zs], c_send.at[1, c], c_recv.at[1, c], (g, t_down)),
        ))
    for copy in x_copies[0]:
        copy.start()
    for c in range(CHUNKS):
        for copy in y_copies[c]:
            copy.start()
    for copy in x_copies[0]:
        copy.wait_send()
    for copy in x_copies[1] + x_copies[2]:
        copy.start()
    for to in in_plane:
        pl.semaphore_signal(ready, inc=1, device_id=to, device_id_type=MESH)
    pl.semaphore_wait(ready, PLANE - 1)

    @pl.loop(1, n_yz)
    def _(i):
        to = lax.rem(t + i * STRIDE, n_yz)
        remote(msg.at[to], slots.at[t], slot_send, slot_recv, (g, to)).start()

    pltpu.make_async_copy(msg.at[t], slots.at[t], slot_recv).start()
    for copy in x_copies[3]:
        copy.start()

    def corners(c):
        zs = pl.ds(c * zc, zc)
        for copy in x_copies[c]:
            copy.wait_recv()
        for side, ref, live in ((0, xb, g > 0), (1, xa, g < n_gx - 1)):
            @pl.when(jnp.logical_not(live))
            def _():
                ref[:, :, zs] = jnp.zeros((6, 8, zc), jnp.float32)

            for q in range(6):
                at = 36 * side + 6 * q
                cup[at : at + 6, zs] = ref[q, 2:8, zs]
                cdown[at : at + 6, zs] = ref[q, 0:6, zs]
        for copy in c_copies[c]:
            copy.start()

    def split(x):
        p1 = x.astype(jnp.bfloat16)
        r = x - p1.astype(jnp.float32)
        p2 = r.astype(jnp.bfloat16)
        return p1, p2, (r - p2.astype(jnp.float32)).astype(jnp.bfloat16)

    def place(ref, size, at, x):
        rows = x.shape[0]
        parts = split(x)
        for i, p in enumerate(PARTS):
            ref[i * size + at : i * size + at + rows, :] = parts[p]

    def first_part(c):
        zs = pl.ds(c * zc, zc)
        place(first_in, FIRST, 0, pot[:, :, zs].reshape(64, zc))
        place(first_in, FIRST, 64, xb[:, :, zs].reshape(48, zc))
        place(first_in, FIRST, 112, xa[:, :, zs].reshape(48, zc))
        partial[:, zs] = jnp.dot(plane_w[:, :KFIRST], first_in[...], preferred_element_type=jnp.float32)

    first_in[6 * FIRST :, :] = jnp.zeros((KFIRST - 6 * FIRST, zc), jnp.bfloat16)
    plane_in.wait()
    band_in.wait()
    for c in range(CHUNKS):
        corners(c)
        first_part(c)

    pltpu.make_async_copy(msg, slots, slot_recv).wait()
    zr = jnp.bitwise_and(slots[:, 1, :] - HALO, 2047)
    window = jnp.right_shift(zr * 565, 16)
    addr_v[...] = slots[:, 0, :] * WINDOWS + window
    to_scalar = pltpu.make_async_copy(addr_v, addr_s, local_sem.at[2])
    to_scalar.start()
    zl = (zr - window * STEP).astype(jnp.float32)
    weight = (slots[:, 2, :].astype(jnp.float32) + 0.5) / BINS
    lane = lax.broadcasted_iota(jnp.int32, (128, 128), 1).astype(jnp.float32)
    columns = jnp.transpose(jnp.concatenate([zl, weight], axis=0))

    def interpolation_rows(homes):
        scale = SIGMA * SIGMA
        for h in homes:
            z_at = columns[:, h : h + 1]
            w_at = columns[:, 64 + h : 65 + h] * scale
            wrow[h] = jnp.where(lane == z_at, scale - w_at, jnp.where(lane == z_at + 1.0, w_at, 0.0))


    flat = tab.reshape(64 * WINDOWS * 8, 128)

    def windows(lo, hi):
        parts = [split(partial[:, 2 * STEP * w : 2 * STEP * w + 256]) for w in range(lo, hi)]
        for a, b, f in GROUPS:
            lhs = jnp.concatenate([jnp.concatenate([g[p][a:b] for p in PARTS], axis=1) for g in parts], axis=0)
            h = jnp.dot(lhs, band_w[f], preferred_element_type=jnp.float32)
            at = 0
            for w in range(lo, hi):
                for comp in range(a // 64, b // 64):
                    for ct in range(8):
                        for half in range(2):
                            v = h[at : at + 8, 128 * half : 128 * half + 128]
                            first = ((8 * ct) * WINDOWS + 2 * w + half) * 8 + comp
                            flat[pl.ds(first, 8, stride=8 * WINDOWS), :] = v
                        at += 8

    def dense(c):
        zs = pl.ds(c * zc, zc)
        for copy in y_copies[c] + c_copies[c]:
            copy.wait_recv()
        first, last = t > 0, t < n_yz - 1
        place(second_in, SECOND, 0, jnp.where(first, yb[:, zs], 0.0))
        place(second_in, SECOND, 48, jnp.where(last, ya[:, zs], 0.0))
        zero8 = jnp.zeros((8, zc), jnp.float32)
        place(second_in, SECOND, 96, jnp.concatenate([jnp.where(first, cb[:, zs], 0.0), zero8], axis=0))
        place(second_in, SECOND, 176, jnp.concatenate([jnp.where(last, ca[:, zs], 0.0), zero8], axis=0))
        field = partial[:, zs] + jnp.dot(plane_w[:, KFIRST:], second_in[...], preferred_element_type=jnp.float32)
        partial[:, zs] = field
        if c == 0:
            partial[:, 2048:2176] = field[:, 0:128]
        lo, hi = 2 * c, 2 * c + (2 if c < CHUNKS - 1 else 3)
        windows(lo, hi)

    interpolation_rows(range(n_yz))
    live[...] = jnp.transpose(jnp.broadcast_to(counts[...], (128, n_yz)))
    for c in range(CHUNKS):
        dense(c)
    to_scalar.wait()
    lane8 = lax.broadcasted_iota(jnp.int32, (8, 128), 1)

    six = pl.ds(0, 6)

    def serve(h):
        acc = jnp.zeros((8, 128), jnp.float32)
        for j in range(128):
            row = addr_s[h, j]
            p = tab[row] * wrow[h, pl.ds(j, 1), :]
            acc = jnp.where(lane8 == j, jnp.sum(p, axis=1, keepdims=True), acc)
        served[h] = acc

    @pl.loop(0, lines)
    def _(i):
        away = lines // 2 + (i + 1) // 2 * (1 - 2 * lax.rem(i, 2))
        homes = [lax.rem(z + away, lines) * PLANE + lax.rem(q + 1 + k, PLANE) for k in range(PLANE)]
        for h in homes:
            serve(h)
        for h in homes:
            @pl.when(h != t)
            def _():
                remote(served.at[h, six], returned.at[t, six], ret_send, ret_recv, (g, h)).start()

            @pl.when(h == t)
            def _():
                pltpu.make_async_copy(served.at[t, six], returned.at[t, six], ret_recv).start()

    pltpu.make_async_copy(served.at[:, six], returned.at[:, six], ret_recv).wait()
    keep = lax.broadcasted_iota(jnp.int32, (n_yz, 128), 1) < live[...]
    for a, at in enumerate(ORDER):
        out[a] = jnp.where(keep, returned[:, at, :], 0.0)
    others = pl.ds(0, n_yz - 1)
    pltpu.make_async_copy(served.at[others, six], returned.at[others, six], ret_send).wait()
    pltpu.make_async_copy(msg.at[pl.ds(0, n_yz - 1)], slots.at[pl.ds(0, n_yz - 1)], slot_send).wait()
    for c in range(CHUNKS):
        for copy in (x_copies[c] if c else ()) + y_copies[c] + c_copies[c]:
            copy.wait_send()


def body(n_gx, n_yz, potential, gal_cells, gal_z, gal_bins, gal_counts):
    tiles, cap = gal_cells.shape[2], gal_cells.shape[3]
    cz = potential.shape[2]
    f32, bf16, i32 = jnp.float32, jnp.bfloat16, jnp.int32
    vmem = pl.BlockSpec(memory_space=pltpu.VMEM)
    hbm = pl.BlockSpec(memory_space=pl.ANY)
    dma = pltpu.SemaphoreType.DMA
    returned = pl.pallas_call(
        functools.partial(kernel, n_gx, n_yz),
        out_shape=jax.ShapeDtypeStruct((6, tiles, cap), f32),
        in_specs=[hbm] * 7,
        out_specs=vmem,
        scratch_shapes=[
            pltpu.VMEM(potential.shape, f32),
            pltpu.VMEM((tiles, cap), i32),
            pltpu.VMEM((tiles, cap), i32),
            pltpu.VMEM((tiles, cap), i32),
            pltpu.VMEM((1, tiles), i32),
            pltpu.VMEM((tiles, 4, cap), i32),
            pltpu.VMEM((tiles, 4, cap), i32),
            pltpu.VMEM((6, 8, cz), f32),
            pltpu.VMEM((6, 8, cz), f32),
            pltpu.VMEM((48, cz), f32),
            pltpu.VMEM((48, cz), f32),
            pltpu.VMEM((72, cz), f32),
            pltpu.VMEM((72, cz), f32),
            pltpu.VMEM((48, cz), f32),
            pltpu.VMEM((48, cz), f32),
            pltpu.VMEM((72, cz), f32),
            pltpu.VMEM((72, cz), f32),
            pltpu.VMEM((384, KFIRST + KSECOND), bf16),
            pltpu.VMEM((3, 1536, 256), bf16),
            pltpu.VMEM((KFIRST, cz // CHUNKS), bf16),
            pltpu.VMEM((KSECOND, cz // CHUNKS), bf16),
            pltpu.VMEM((384, cz + 128), f32),
            pltpu.VMEM((64 * WINDOWS, 8, 128), f32),
            pltpu.VMEM((tiles, cap, 128), f32),
            pltpu.VMEM((tiles, cap), i32),
            pltpu.SMEM((tiles, cap), i32),
            pltpu.VMEM((tiles, 8, cap), f32),
            pltpu.VMEM((tiles, 8, cap), f32),
            pltpu.VMEM((tiles, cap), i32),
            dma((3,)),
            dma((5,)),
            pltpu.SemaphoreType.REGULAR,
            dma,
            dma,
            dma((2, CHUNKS)),
            dma((2, CHUNKS)),
            dma((2, CHUNKS)),
            dma((2, CHUNKS)),
            dma((2, CHUNKS)),
            dma((2, CHUNKS)),
            dma,
            dma,
        ],
        compiler_params=pltpu.CompilerParams(
            collective_id=0, has_side_effects=True, vmem_limit_bytes=60 * 1024 * 1024
        ),
        name="tidal",
    )(
        potential,
        gal_cells.reshape(tiles, cap),
        gal_z.reshape(tiles, cap),
        gal_bins.reshape(tiles, cap),
        gal_counts.reshape(1, tiles),
        jnp.asarray(plane_weights()),
        jnp.asarray(band_weights()),
    )
    return returned.reshape(6, 1, 1, tiles * cap)


def solution(mesh):
    return jax.shard_map(
        functools.partial(body, mesh.shape["gx"], mesh.shape["yz"]),
        mesh=mesh,
        in_specs=(
            P("gx", "yz", None),
            P("gx", "yz", None, None),
            P("gx", "yz", None, None),
            P("gx", "yz", None, None),
            P("gx", "yz", None),
        ),
        out_specs=P(None, "gx", "yz", None),
        check_vma=False,
    )
```

```python
import functools

import jax
import jax.numpy as jnp
import ml_dtypes
import numpy as np
from jax import lax
from jax.experimental import pallas as pl
from jax.experimental.pallas import tpu as pltpu
from jax.sharding import PartitionSpec as P

HALO = 6
BINS = 8
SIGMA = HALO / 3.0
STEP = 116
MESH = pl.DeviceIdType.MESH
CHUNKS = 4
PLANE = 8
STRIDE = 1
WINDOWS = 19
FIRST = 160
SECOND = 256
KROWS = FIRST + SECOND
KFIRST, KSECOND = 1024, 6 * SECOND
PARTS = (0, 1, 2, 0, 1, 0)
WEIGHT_PARTS = (0, 0, 0, 1, 1, 2)
ORDER = (0, 1, 5, 2, 3, 4)
GROUPS = ((0, 192, 0), (192, 320, 1), (320, 384, 2))


def filters():
    k = np.arange(-HALO, HALO + 1).astype(np.float64)
    w0 = np.exp(-k * k / (2.0 * SIGMA * SIGMA))
    w0 = w0 / w0.sum()
    return w0, k / SIGMA**2 * w0, (k * k / SIGMA**4 - 1.0 / SIGMA**2) * w0


def split3(a):
    parts = []
    for _ in range(3):
        p = a.astype(ml_dtypes.bfloat16)
        parts.append(p)
        a = a - p.astype(np.float64)
    return parts


def plane_weights():
    w = filters()
    rows = [(x, y) for x in range(8) for y in range(8)]
    rows += [(x, y) for x in range(-6, 0) for y in range(8)]
    rows += [(x, y) for x in range(8, 14) for y in range(8)]
    rows += [(x, y) for x in range(8) for y in range(-6, 0)]
    rows += [(x, y) for x in range(8) for y in range(8, 14)]
    outer = list(range(-6, 0)) + list(range(8, 14))
    for ys in (range(-6, 0), range(8, 14)):
        rows += [(x, y) for x in outer for y in ys] + [None] * 8
    pairs = ((2, 0), (0, 2), (1, 1), (1, 0), (0, 1), (0, 0))
    a = np.zeros((6, 8, 8, KROWS))
    for k, at in enumerate(rows):
        if at is None:
            continue
        for xo in range(8):
            dx = at[0] - xo + HALO
            for yo in range(8):
                dy = at[1] - yo + HALO
                if 0 <= dx <= 2 * HALO and 0 <= dy <= 2 * HALO:
                    for c, (fx, fy) in enumerate(pairs):
                        a[c, xo, yo, k] = w[fx][dx] * w[fy][dy]
    parts = split3(a.reshape(384, KROWS))
    out = np.zeros((384, KFIRST + KSECOND), ml_dtypes.bfloat16)
    for i, p in enumerate(WEIGHT_PARTS):
        out[:, i * FIRST : (i + 1) * FIRST] = parts[p][:, :FIRST]
        at = KFIRST + i * SECOND
        out[:, at : at + SECOND] = parts[p][:, FIRST:]
    return out


def band_weights():
    w = filters()
    out = np.zeros((3, 6 * 256, 256), ml_dtypes.bfloat16)
    for f in range(3):
        band = np.zeros((256, 256))
        for half in range(2):
            for lane in range(128):
                for tap in range(2 * HALO + 1):
                    band[half * STEP + lane + tap, half * 128 + lane] = w[f][tap]
        parts = split3(band)
        for i, p in enumerate(WEIGHT_PARTS):
            out[f, i * 256 : (i + 1) * 256] = parts[p]
    return out


def kernel(
    n_gx, n_yz, pot_hbm, cells_hbm, zeds_hbm, bins_hbm, counts_hbm, plane_hbm, band_hbm, out,
    pot, cells, zeds, bins, counts, msg, slots, xb, xa, up, down, cup, cdown, yb, ya, cb, ca,
    plane_w, band_w, first_in, second_in, partial, tab, wrow, addr_v, addr_s, served, returned, live,
    local_sem, in_sem, ready, slot_send, slot_recv, x_send, x_recv, y_send, y_recv, c_send, c_recv, ret_send, ret_recv,
):
    g = lax.axis_index("gx")
    t = lax.axis_index("yz")
    zc = pot.shape[2] // CHUNKS
    g_up, g_down = lax.rem(g + 1, n_gx), lax.rem(g + n_gx - 1, n_gx)
    t_up, t_down = lax.rem(t + 1, n_yz), lax.rem(t + n_yz - 1, n_yz)

    barrier = pltpu.get_barrier_semaphore()

    z, q = t // PLANE, lax.rem(t, PLANE)
    lines = n_yz // PLANE
    in_plane = [(g, z * PLANE + lax.rem(q + i, PLANE)) for i in range(1, PLANE)]
    in_line = [(g, lax.rem(z + i, lines) * PLANE + q) for i in range(1, lines)]
    for to in [(g_up, t), (g_down, t)] + in_plane + in_line:
        pl.semaphore_signal(barrier, inc=1, device_id=to, device_id_type=MESH)

    @pl.when(q == PLANE - 1)
    def _():
        pl.semaphore_signal(barrier, inc=1, device_id=(g, t_up), device_id_type=MESH)

    @pl.when(q == 0)
    def _():
        pl.semaphore_signal(barrier, inc=1, device_id=(g, t_down), device_id_type=MESH)

    loads = [
        pltpu.make_async_copy(src, dst, in_sem.at[i])
        for i, (src, dst) in enumerate(
            ((pot_hbm, pot), (cells_hbm, cells), (zeds_hbm, zeds), (bins_hbm, bins), (counts_hbm, counts))
        )
    ]
    for load in loads:
        load.start()
    plane_in = pltpu.make_async_copy(plane_hbm, plane_w, local_sem.at[0])
    band_in = pltpu.make_async_copy(band_hbm, band_w, local_sem.at[1])
    plane_in.start()
    band_in.start()
    for load in loads:
        load.wait()
    for i, ref in enumerate((cells, zeds, bins)):
        msg[:, i, :] = ref[...]
    for p in range(8):
        up[6 * p : 6 * p + 6, :] = pot[p, 2:8, :]
        down[6 * p : 6 * p + 6, :] = pot[p, 0:6, :]
    edge = jnp.logical_or(q == PLANE - 1, q == 0)

    @pl.when(edge)
    def _():
        pl.semaphore_wait(barrier, PLANE + lines + 1)

    @pl.when(jnp.logical_not(edge))
    def _():
        pl.semaphore_wait(barrier, PLANE + lines)

    def remote(src, dst, send, recv, to):
        return pltpu.make_async_remote_copy(
            src_ref=src, dst_ref=dst, send_sem=send, recv_sem=recv, device_id=to, device_id_type=MESH
        )

    x_copies, y_copies, c_copies = [], [], []
    for c in range(CHUNKS):
        zs = pl.ds(c * zc, zc)
        x_copies.append((
            remote(pot.at[pl.ds(2, 6), :, zs], xb.at[:, :, zs], x_send.at[0, c], x_recv.at[0, c], (g_up, t)),
            remote(pot.at[pl.ds(0, 6), :, zs], xa.at[:, :, zs], x_send.at[1, c], x_recv.at[1, c], (g_down, t)),
        ))
        y_copies.append((
            remote(up.at[:, zs], yb.at[:, zs], y_send.at[0, c], y_recv.at[0, c], (g, t_up)),
            remote(down.at[:, zs], ya.at[:, zs], y_send.at[1, c], y_recv.at[1, c], (g, t_down)),
        ))
        c_copies.append((
            remote(cup.at[:, zs], cb.at[:, zs], c_send.at[0, c], c_recv.at[0, c], (g, t_up)),
            remote(cdown.at[:, zs], ca.at[:, zs], c_send.at[1, c], c_recv.at[1, c], (g, t_down)),
        ))
    for copy in x_copies[0]:
        copy.start()
    for c in range(CHUNKS):
        for copy in y_copies[c]:
            copy.start()
    for copy in x_copies[0]:
        copy.wait_send()
    for copy in x_copies[1] + x_copies[2]:
        copy.start()
    for to in in_plane:
        pl.semaphore_signal(ready, inc=1, device_id=to, device_id_type=MESH)
    pl.semaphore_wait(ready, PLANE - 1)

    @pl.loop(1, n_yz)
    def _(i):
        to = lax.rem(t + i * STRIDE, n_yz)
        remote(msg.at[to], slots.at[t], slot_send, slot_recv, (g, to)).start()

    pltpu.make_async_copy(msg.at[t], slots.at[t], slot_recv).start()
    for copy in x_copies[3]:
        copy.start()

    def corners(c):
        zs = pl.ds(c * zc, zc)
        for copy in x_copies[c]:
            copy.wait_recv()
        for side, ref, live in ((0, xb, g > 0), (1, xa, g < n_gx - 1)):
            @pl.when(jnp.logical_not(live))
            def _():
                ref[:, :, zs] = jnp.zeros((6, 8, zc), jnp.float32)

            for q in range(6):
                at = 36 * side + 6 * q
                cup[at : at + 6, zs] = ref[q, 2:8, zs]
                cdown[at : at + 6, zs] = ref[q, 0:6, zs]
        for copy in c_copies[c]:
            copy.start()

    def split(x):
        p1 = x.astype(jnp.bfloat16)
        r = x - p1.astype(jnp.float32)
        p2 = r.astype(jnp.bfloat16)
        return p1, p2, (r - p2.astype(jnp.float32)).astype(jnp.bfloat16)

    def place(ref, size, at, x):
        rows = x.shape[0]
        parts = split(x)
        for i, p in enumerate(PARTS):
            ref[i * size + at : i * size + at + rows, :] = parts[p]

    def first_part(c):
        zs = pl.ds(c * zc, zc)
        place(first_in, FIRST, 0, pot[:, :, zs].reshape(64, zc))
        place(first_in, FIRST, 64, xb[:, :, zs].reshape(48, zc))
        place(first_in, FIRST, 112, xa[:, :, zs].reshape(48, zc))
        partial[:, zs] = jnp.dot(plane_w[:, :KFIRST], first_in[...], preferred_element_type=jnp.float32)

    first_in[6 * FIRST :, :] = jnp.zeros((KFIRST - 6 * FIRST, zc), jnp.bfloat16)
    plane_in.wait()
    band_in.wait()
    for c in range(CHUNKS - 1):
        corners(c)
        first_part(c)

    pltpu.make_async_copy(msg, slots, slot_recv).wait()
    zr = jnp.bitwise_and(slots[:, 1, :] - HALO, 2047)
    window = jnp.right_shift(zr * 565, 16)
    addr_v[...] = slots[:, 0, :] * WINDOWS + window
    to_scalar = pltpu.make_async_copy(addr_v, addr_s, local_sem.at[2])
    to_scalar.start()
    zl = (zr - window * STEP).astype(jnp.float32)
    weight = (slots[:, 2, :].astype(jnp.float32) + 0.5) / BINS
    lane = lax.broadcasted_iota(jnp.int32, (128, 128), 1).astype(jnp.float32)
    columns = jnp.transpose(jnp.concatenate([zl, weight], axis=0))

    def interpolation_rows(homes):
        scale = SIGMA * SIGMA
        for h in homes:
            z_at = columns[:, h : h + 1]
            w_at = columns[:, 64 + h : 65 + h] * scale
            wrow[h] = jnp.where(lane == z_at, scale - w_at, jnp.where(lane == z_at + 1.0, w_at, 0.0))

    interpolation_rows(range(n_yz // 2))
    corners(3)
    first_part(3)
    flat = tab.reshape(64 * WINDOWS * 8, 128)

    def windows(lo, hi):
        parts = [split(partial[:, 2 * STEP * w : 2 * STEP * w + 256]) for w in range(lo, hi)]
        for a, b, f in GROUPS:
            lhs = jnp.concatenate([jnp.concatenate([g[p][a:b] for p in PARTS], axis=1) for g in parts], axis=0)
            h = jnp.dot(lhs, band_w[f], preferred_element_type=jnp.float32)
            at = 0
            for w in range(lo, hi):
                for comp in range(a // 64, b // 64):
                    for ct in range(8):
                        for half in range(2):
                            v = h[at : at + 8, 128 * half : 128 * half + 128]
                            first = ((8 * ct) * WINDOWS + 2 * w + half) * 8 + comp
                            flat[pl.ds(first, 8, stride=8 * WINDOWS), :] = v
                        at += 8

    def dense(c):
        zs = pl.ds(c * zc, zc)
        for copy in y_copies[c] + c_copies[c]:
            copy.wait_recv()
        first, last = t > 0, t < n_yz - 1
        place(second_in, SECOND, 0, jnp.where(first, yb[:, zs], 0.0))
        place(second_in, SECOND, 48, jnp.where(last, ya[:, zs], 0.0))
        zero8 = jnp.zeros((8, zc), jnp.float32)
        place(second_in, SECOND, 96, jnp.concatenate([jnp.where(first, cb[:, zs], 0.0), zero8], axis=0))
        place(second_in, SECOND, 176, jnp.concatenate([jnp.where(last, ca[:, zs], 0.0), zero8], axis=0))
        field = partial[:, zs] + jnp.dot(plane_w[:, KFIRST:], second_in[...], preferred_element_type=jnp.float32)
        partial[:, zs] = field
        if c == 0:
            partial[:, 2048:2176] = field[:, 0:128]
        lo, hi = 2 * c, 2 * c + (2 if c < CHUNKS - 1 else 3)
        windows(lo, hi)

    interpolation_rows(range(n_yz // 2, n_yz))
    live[...] = jnp.transpose(jnp.broadcast_to(counts[...], (128, n_yz)))
    for c in range(CHUNKS):
        dense(c)
    to_scalar.wait()
    lane8 = lax.broadcasted_iota(jnp.int32, (8, 128), 1)

    six = pl.ds(0, 6)

    def serve(h):
        acc = jnp.zeros((8, 128), jnp.float32)
        for j in range(128):
            row = addr_s[h, j]
            p = tab[row] * wrow[h, pl.ds(j, 1), :]
            acc = jnp.where(lane8 == j, jnp.sum(p, axis=1, keepdims=True), acc)
        served[h] = acc

    def serve_line(i, count):
        away = lines // 2 + (i + 1) // 2 * (1 - 2 * lax.rem(i, 2))
        homes = [lax.rem(z + away, lines) * PLANE + lax.rem(q + 1 + k, PLANE) for k in range(PLANE)]
        for h in homes:
            serve(h)
        for h in homes[:count]:
            remote(served.at[h, six], returned.at[t, six], ret_send, ret_recv, (g, h)).start()

    @pl.loop(0, lines - 1)
    def _(i):
        serve_line(i, PLANE)

    serve_line(lines - 1, PLANE - 1)
    pltpu.make_async_copy(served.at[t, six], returned.at[t, six], ret_recv).start()

    pltpu.make_async_copy(served.at[:, six], returned.at[:, six], ret_recv).wait()
    keep = lax.broadcasted_iota(jnp.int32, (n_yz, 128), 1) < live[...]
    for a, at in enumerate(ORDER):
        out[a] = jnp.where(keep, returned[:, at, :], 0.0)
    others = pl.ds(0, n_yz - 1)
    pltpu.make_async_copy(served.at[others, six], returned.at[others, six], ret_send).wait()
    pltpu.make_async_copy(msg.at[pl.ds(0, n_yz - 1)], slots.at[pl.ds(0, n_yz - 1)], slot_send).wait()
    for c in range(CHUNKS):
        for copy in (x_copies[c] if c else ()) + y_copies[c] + c_copies[c]:
            copy.wait_send()


def body(n_gx, n_yz, potential, gal_cells, gal_z, gal_bins, gal_counts):
    tiles, cap = gal_cells.shape[2], gal_cells.shape[3]
    cz = potential.shape[2]
    f32, bf16, i32 = jnp.float32, jnp.bfloat16, jnp.int32
    vmem = pl.BlockSpec(memory_space=pltpu.VMEM)
    hbm = pl.BlockSpec(memory_space=pl.ANY)
    dma = pltpu.SemaphoreType.DMA
    returned = pl.pallas_call(
        functools.partial(kernel, n_gx, n_yz),
        out_shape=jax.ShapeDtypeStruct((6, tiles, cap), f32),
        in_specs=[hbm] * 7,
        out_specs=vmem,
        scratch_shapes=[
            pltpu.VMEM(potential.shape, f32),
            pltpu.VMEM((tiles, cap), i32),
            pltpu.VMEM((tiles, cap), i32),
            pltpu.VMEM((tiles, cap), i32),
            pltpu.VMEM((1, tiles), i32),
            pltpu.VMEM((tiles, 4, cap), i32),
            pltpu.VMEM((tiles, 4, cap), i32),
            pltpu.VMEM((6, 8, cz), f32),
            pltpu.VMEM((6, 8, cz), f32),
            pltpu.VMEM((48, cz), f32),
            pltpu.VMEM((48, cz), f32),
            pltpu.VMEM((72, cz), f32),
            pltpu.VMEM((72, cz), f32),
            pltpu.VMEM((48, cz), f32),
            pltpu.VMEM((48, cz), f32),
            pltpu.VMEM((72, cz), f32),
            pltpu.VMEM((72, cz), f32),
            pltpu.VMEM((384, KFIRST + KSECOND), bf16),
            pltpu.VMEM((3, 1536, 256), bf16),
            pltpu.VMEM((KFIRST, cz // CHUNKS), bf16),
            pltpu.VMEM((KSECOND, cz // CHUNKS), bf16),
            pltpu.VMEM((384, cz + 128), f32),
            pltpu.VMEM((64 * WINDOWS, 8, 128), f32),
            pltpu.VMEM((tiles, cap, 128), f32),
            pltpu.VMEM((tiles, cap), i32),
            pltpu.SMEM((tiles, cap), i32),
            pltpu.VMEM((tiles, 8, cap), f32),
            pltpu.VMEM((tiles, 8, cap), f32),
            pltpu.VMEM((tiles, cap), i32),
            dma((3,)),
            dma((5,)),
            pltpu.SemaphoreType.REGULAR,
            dma,
            dma,
            dma((2, CHUNKS)),
            dma((2, CHUNKS)),
            dma((2, CHUNKS)),
            dma((2, CHUNKS)),
            dma((2, CHUNKS)),
            dma((2, CHUNKS)),
            dma,
            dma,
        ],
        compiler_params=pltpu.CompilerParams(
            collective_id=0, has_side_effects=True, vmem_limit_bytes=60 * 1024 * 1024
        ),
        name="tidal",
    )(
        potential,
        gal_cells.reshape(tiles, cap),
        gal_z.reshape(tiles, cap),
        gal_bins.reshape(tiles, cap),
        gal_counts.reshape(1, tiles),
        jnp.asarray(plane_weights()),
        jnp.asarray(band_weights()),
    )
    return returned.reshape(6, 1, 1, tiles * cap)


def solution(mesh):
    return jax.shard_map(
        functools.partial(body, mesh.shape["gx"], mesh.shape["yz"]),
        mesh=mesh,
        in_specs=(
            P("gx", "yz", None),
            P("gx", "yz", None, None),
            P("gx", "yz", None, None),
            P("gx", "yz", None, None),
            P("gx", "yz", None),
        ),
        out_specs=P(None, "gx", "yz", None),
        check_vma=False,
    )
```

```python
import functools

import jax
import jax.numpy as jnp
import ml_dtypes
import numpy as np
from jax import lax
from jax.experimental import pallas as pl
from jax.experimental.pallas import tpu as pltpu
from jax.sharding import PartitionSpec as P

HALO = 6
BINS = 8
SIGMA = HALO / 3.0
STEP = 116
MESH = pl.DeviceIdType.MESH
CHUNKS = 4
PLANE = 8
STRIDE = 1
WINDOWS = 19
FIRST = 256
SECOND = 160
KROWS = FIRST + SECOND
KFIRST, KSECOND = 6 * FIRST, 1024
PARTS = (0, 1, 2, 0, 1, 0)
WEIGHT_PARTS = (0, 0, 0, 1, 1, 2)
ORDER = (0, 1, 5, 2, 3, 4)
GROUPS = ((0, 192, 0), (192, 320, 1), (320, 384, 2))


def filters():
    k = np.arange(-HALO, HALO + 1).astype(np.float64)
    w0 = np.exp(-k * k / (2.0 * SIGMA * SIGMA))
    w0 = w0 / w0.sum()
    return w0, k / SIGMA**2 * w0, (k * k / SIGMA**4 - 1.0 / SIGMA**2) * w0


def split3(a):
    parts = []
    for _ in range(3):
        p = a.astype(ml_dtypes.bfloat16)
        parts.append(p)
        a = a - p.astype(np.float64)
    return parts


def plane_weights():
    w = filters()
    rows = [(x, y) for x in range(8) for y in range(8)]
    rows += [(x, y) for x in range(-6, 0) for y in range(8)]
    rows += [(x, y) for x in range(8, 14) for y in range(8)]
    rows += [(x, y) for x in range(8) for y in range(-6, 0)]
    rows += [(x, y) for x in range(8) for y in range(8, 14)]
    outer = list(range(-6, 0)) + list(range(8, 14))
    for ys in (range(-6, 0), range(8, 14)):
        rows += [(x, y) for x in outer for y in ys] + [None] * 8
    pairs = ((2, 0), (0, 2), (1, 1), (1, 0), (0, 1), (0, 0))
    a = np.zeros((6, 8, 8, KROWS))
    for k, at in enumerate(rows):
        if at is None:
            continue
        for xo in range(8):
            dx = at[0] - xo + HALO
            for yo in range(8):
                dy = at[1] - yo + HALO
                if 0 <= dx <= 2 * HALO and 0 <= dy <= 2 * HALO:
                    for c, (fx, fy) in enumerate(pairs):
                        a[c, xo, yo, k] = w[fx][dx] * w[fy][dy]
    parts = split3(a.reshape(384, KROWS))
    out = np.zeros((384, KFIRST + KSECOND), ml_dtypes.bfloat16)
    for i, p in enumerate(WEIGHT_PARTS):
        out[:, i * FIRST : (i + 1) * FIRST] = parts[p][:, :FIRST]
        at = KFIRST + i * SECOND
        out[:, at : at + SECOND] = parts[p][:, FIRST:]
    return out


def band_weights():
    w = filters()
    out = np.zeros((3, 6 * 256, 256), ml_dtypes.bfloat16)
    for f in range(3):
        band = np.zeros((256, 256))
        for half in range(2):
            for lane in range(128):
                for tap in range(2 * HALO + 1):
                    band[half * STEP + lane + tap, half * 128 + lane] = w[f][tap]
        parts = split3(band)
        for i, p in enumerate(WEIGHT_PARTS):
            out[f, i * 256 : (i + 1) * 256] = parts[p]
    return out


def kernel(
    n_gx, n_yz, pot_hbm, cells_hbm, zeds_hbm, bins_hbm, counts_hbm, plane_hbm, band_hbm, out,
    pot, cells, zeds, bins, counts, msg, slots, xb, xa, up, down, cup, cdown, yb, ya, cb, ca,
    plane_w, band_w, first_in, second_in, partial, tab, wrow, addr_v, addr_s, served, returned, live,
    local_sem, in_sem, ready, slot_send, slot_recv, x_send, x_recv, y_send, y_recv, c_send, c_recv, ret_send, ret_recv,
):
    g = lax.axis_index("gx")
    t = lax.axis_index("yz")
    zc = pot.shape[2] // CHUNKS
    g_up, g_down = lax.rem(g + 1, n_gx), lax.rem(g + n_gx - 1, n_gx)
    t_up, t_down = lax.rem(t + 1, n_yz), lax.rem(t + n_yz - 1, n_yz)

    barrier = pltpu.get_barrier_semaphore()

    z, q = t // PLANE, lax.rem(t, PLANE)
    lines = n_yz // PLANE
    in_plane = [(g, z * PLANE + lax.rem(q + i, PLANE)) for i in range(1, PLANE)]
    in_line = [(g, lax.rem(z + i, lines) * PLANE + q) for i in range(1, lines)]
    for to in [(g_up, t), (g_down, t)] + in_plane + in_line:
        pl.semaphore_signal(barrier, inc=1, device_id=to, device_id_type=MESH)

    @pl.when(q == PLANE - 1)
    def _():
        pl.semaphore_signal(barrier, inc=1, device_id=(g, t_up), device_id_type=MESH)

    @pl.when(q == 0)
    def _():
        pl.semaphore_signal(barrier, inc=1, device_id=(g, t_down), device_id_type=MESH)

    loads = [
        pltpu.make_async_copy(src, dst, in_sem.at[i])
        for i, (src, dst) in enumerate(
            ((pot_hbm, pot), (cells_hbm, cells), (zeds_hbm, zeds), (bins_hbm, bins), (counts_hbm, counts))
        )
    ]
    for load in loads:
        load.start()
    plane_in = pltpu.make_async_copy(plane_hbm, plane_w, local_sem.at[0])
    band_in = pltpu.make_async_copy(band_hbm, band_w, local_sem.at[1])
    plane_in.start()
    band_in.start()
    for load in loads:
        load.wait()
    for i, ref in enumerate((cells, zeds, bins)):
        msg[:, i, :] = ref[...]
    for p in range(8):
        up[6 * p : 6 * p + 6, :] = pot[p, 2:8, :]
        down[6 * p : 6 * p + 6, :] = pot[p, 0:6, :]
    edge = jnp.logical_or(q == PLANE - 1, q == 0)

    @pl.when(edge)
    def _():
        pl.semaphore_wait(barrier, PLANE + lines + 1)

    @pl.when(jnp.logical_not(edge))
    def _():
        pl.semaphore_wait(barrier, PLANE + lines)

    def remote(src, dst, send, recv, to):
        return pltpu.make_async_remote_copy(
            src_ref=src, dst_ref=dst, send_sem=send, recv_sem=recv, device_id=to, device_id_type=MESH
        )

    x_copies, y_copies, c_copies = [], [], []
    for c in range(CHUNKS):
        zs = pl.ds(c * zc, zc)
        x_copies.append((
            remote(pot.at[pl.ds(2, 6), :, zs], xb.at[:, :, zs], x_send.at[0, c], x_recv.at[0, c], (g_up, t)),
            remote(pot.at[pl.ds(0, 6), :, zs], xa.at[:, :, zs], x_send.at[1, c], x_recv.at[1, c], (g_down, t)),
        ))
        y_copies.append((
            remote(up.at[:, zs], yb.at[:, zs], y_send.at[0, c], y_recv.at[0, c], (g, t_up)),
            remote(down.at[:, zs], ya.at[:, zs], y_send.at[1, c], y_recv.at[1, c], (g, t_down)),
        ))
        c_copies.append((
            remote(cup.at[:, zs], cb.at[:, zs], c_send.at[0, c], c_recv.at[0, c], (g, t_up)),
            remote(cdown.at[:, zs], ca.at[:, zs], c_send.at[1, c], c_recv.at[1, c], (g, t_down)),
        ))
    for copy in x_copies[0]:
        copy.start()
    for c in range(CHUNKS):
        for copy in y_copies[c]:
            copy.start()
    for copy in x_copies[0]:
        copy.wait_send()
    for copy in x_copies[1] + x_copies[2]:
        copy.start()
    for to in in_plane:
        pl.semaphore_signal(ready, inc=1, device_id=to, device_id_type=MESH)
    pl.semaphore_wait(ready, PLANE - 1)

    @pl.loop(1, n_yz)
    def _(i):
        to = lax.rem(t + i * STRIDE, n_yz)
        remote(msg.at[to], slots.at[t], slot_send, slot_recv, (g, to)).start()

    pltpu.make_async_copy(msg.at[t], slots.at[t], slot_recv).start()
    for copy in x_copies[3]:
        copy.start()

    def corners(c):
        zs = pl.ds(c * zc, zc)
        for copy in x_copies[c]:
            copy.wait_recv()
        for side, ref, live in ((0, xb, g > 0), (1, xa, g < n_gx - 1)):
            @pl.when(jnp.logical_not(live))
            def _():
                ref[:, :, zs] = jnp.zeros((6, 8, zc), jnp.float32)

            for q in range(6):
                at = 36 * side + 6 * q
                cup[at : at + 6, zs] = ref[q, 2:8, zs]
                cdown[at : at + 6, zs] = ref[q, 0:6, zs]
        for copy in c_copies[c]:
            copy.start()

    def split(x):
        p1 = x.astype(jnp.bfloat16)
        r = x - p1.astype(jnp.float32)
        p2 = r.astype(jnp.bfloat16)
        return p1, p2, (r - p2.astype(jnp.float32)).astype(jnp.bfloat16)

    def place(ref, size, at, x):
        rows = x.shape[0]
        parts = split(x)
        for i, p in enumerate(PARTS):
            ref[i * size + at : i * size + at + rows, :] = parts[p]

    def first_part(c):
        zs = pl.ds(c * zc, zc)
        place(first_in, FIRST, 0, pot[:, :, zs].reshape(64, zc))
        place(first_in, FIRST, 64, xb[:, :, zs].reshape(48, zc))
        place(first_in, FIRST, 112, xa[:, :, zs].reshape(48, zc))
        for copy in y_copies[c]:
            copy.wait_recv()
        place(first_in, FIRST, 160, jnp.where(t > 0, yb[:, zs], 0.0))
        place(first_in, FIRST, 208, jnp.where(t < n_yz - 1, ya[:, zs], 0.0))
        partial[:, zs] = jnp.dot(plane_w[:, :KFIRST], first_in[...], preferred_element_type=jnp.float32)

    second_in[6 * SECOND :, :] = jnp.zeros((KSECOND - 6 * SECOND, zc), jnp.bfloat16)
    plane_in.wait()
    band_in.wait()
    for c in range(CHUNKS - 1):
        corners(c)
        first_part(c)

    pltpu.make_async_copy(msg, slots, slot_recv).wait()
    zr = jnp.bitwise_and(slots[:, 1, :] - HALO, 2047)
    window = jnp.right_shift(zr * 565, 16)
    addr_v[...] = slots[:, 0, :] * WINDOWS + window
    to_scalar = pltpu.make_async_copy(addr_v, addr_s, local_sem.at[2])
    to_scalar.start()
    zl = (zr - window * STEP).astype(jnp.float32)
    weight = (slots[:, 2, :].astype(jnp.float32) + 0.5) / BINS
    lane = lax.broadcasted_iota(jnp.int32, (128, 128), 1).astype(jnp.float32)
    columns = jnp.transpose(jnp.concatenate([zl, weight], axis=0))

    def interpolation_rows(homes):
        scale = SIGMA * SIGMA
        for h in homes:
            z_at = columns[:, h : h + 1]
            w_at = columns[:, 64 + h : 65 + h] * scale
            wrow[h] = jnp.where(lane == z_at, scale - w_at, jnp.where(lane == z_at + 1.0, w_at, 0.0))

    interpolation_rows(range(n_yz // 2))
    corners(3)
    first_part(3)
    flat = tab.reshape(64 * WINDOWS * 8, 128)

    def windows(lo, hi):
        parts = [split(partial[:, 2 * STEP * w : 2 * STEP * w + 256]) for w in range(lo, hi)]
        for a, b, f in GROUPS:
            lhs = jnp.concatenate([jnp.concatenate([g[p][a:b] for p in PARTS], axis=1) for g in parts], axis=0)
            h = jnp.dot(lhs, band_w[f], preferred_element_type=jnp.float32)
            at = 0
            for w in range(lo, hi):
                for comp in range(a // 64, b // 64):
                    for ct in range(8):
                        for half in range(2):
                            v = h[at : at + 8, 128 * half : 128 * half + 128]
                            first = ((8 * ct) * WINDOWS + 2 * w + half) * 8 + comp
                            flat[pl.ds(first, 8, stride=8 * WINDOWS), :] = v
                        at += 8

    def dense(c):
        zs = pl.ds(c * zc, zc)
        for copy in c_copies[c]:
            copy.wait_recv()
        first, last = t > 0, t < n_yz - 1
        zero8 = jnp.zeros((8, zc), jnp.float32)
        place(second_in, SECOND, 0, jnp.concatenate([jnp.where(first, cb[:, zs], 0.0), zero8], axis=0))
        place(second_in, SECOND, 80, jnp.concatenate([jnp.where(last, ca[:, zs], 0.0), zero8], axis=0))
        field = partial[:, zs] + jnp.dot(plane_w[:, KFIRST:], second_in[...], preferred_element_type=jnp.float32)
        partial[:, zs] = field
        if c == 0:
            partial[:, 2048:2176] = field[:, 0:128]
        lo, hi = 2 * c, 2 * c + (2 if c < CHUNKS - 1 else 3)
        windows(lo, hi)

    live[...] = jnp.transpose(jnp.broadcast_to(counts[...], (128, n_yz)))
    for c in range(CHUNKS - 1):
        dense(c)
    interpolation_rows(range(n_yz // 2, n_yz))
    dense(CHUNKS - 1)
    to_scalar.wait()
    lane8 = lax.broadcasted_iota(jnp.int32, (8, 128), 1)

    six = pl.ds(0, 6)

    def serve(h):
        acc = jnp.zeros((8, 128), jnp.float32)
        for j in range(128):
            row = addr_s[h, j]
            p = tab[row] * wrow[h, pl.ds(j, 1), :]
            acc = jnp.where(lane8 == j, jnp.sum(p, axis=1, keepdims=True), acc)
        served[h] = acc

    def serve_line(i, count):
        away = lines // 2 + (i + 1) // 2 * (1 - 2 * lax.rem(i, 2))
        homes = [lax.rem(z + away, lines) * PLANE + lax.rem(q + 1 + k, PLANE) for k in range(PLANE)]
        for h in homes:
            serve(h)
        for h in homes[:count]:
            remote(served.at[h, six], returned.at[t, six], ret_send, ret_recv, (g, h)).start()

    @pl.loop(0, lines - 1)
    def _(i):
        serve_line(i, PLANE)

    serve_line(lines - 1, PLANE - 1)
    pltpu.make_async_copy(served.at[t, six], returned.at[t, six], ret_recv).start()

    pltpu.make_async_copy(served.at[:, six], returned.at[:, six], ret_recv).wait()
    keep = lax.broadcasted_iota(jnp.int32, (n_yz, 128), 1) < live[...]
    for a, at in enumerate(ORDER):
        out[a] = jnp.where(keep, returned[:, at, :], 0.0)
    others = pl.ds(0, n_yz - 1)
    pltpu.make_async_copy(served.at[others, six], returned.at[others, six], ret_send).wait()
    pltpu.make_async_copy(msg.at[pl.ds(0, n_yz - 1)], slots.at[pl.ds(0, n_yz - 1)], slot_send).wait()
    for c in range(CHUNKS):
        for copy in (x_copies[c] if c else ()) + y_copies[c] + c_copies[c]:
            copy.wait_send()


def body(n_gx, n_yz, potential, gal_cells, gal_z, gal_bins, gal_counts):
    tiles, cap = gal_cells.shape[2], gal_cells.shape[3]
    cz = potential.shape[2]
    f32, bf16, i32 = jnp.float32, jnp.bfloat16, jnp.int32
    vmem = pl.BlockSpec(memory_space=pltpu.VMEM)
    hbm = pl.BlockSpec(memory_space=pl.ANY)
    dma = pltpu.SemaphoreType.DMA
    returned = pl.pallas_call(
        functools.partial(kernel, n_gx, n_yz),
        out_shape=jax.ShapeDtypeStruct((6, tiles, cap), f32),
        in_specs=[hbm] * 7,
        out_specs=vmem,
        scratch_shapes=[
            pltpu.VMEM(potential.shape, f32),
            pltpu.VMEM((tiles, cap), i32),
            pltpu.VMEM((tiles, cap), i32),
            pltpu.VMEM((tiles, cap), i32),
            pltpu.VMEM((1, tiles), i32),
            pltpu.VMEM((tiles, 4, cap), i32),
            pltpu.VMEM((tiles, 4, cap), i32),
            pltpu.VMEM((6, 8, cz), f32),
            pltpu.VMEM((6, 8, cz), f32),
            pltpu.VMEM((48, cz), f32),
            pltpu.VMEM((48, cz), f32),
            pltpu.VMEM((72, cz), f32),
            pltpu.VMEM((72, cz), f32),
            pltpu.VMEM((48, cz), f32),
            pltpu.VMEM((48, cz), f32),
            pltpu.VMEM((72, cz), f32),
            pltpu.VMEM((72, cz), f32),
            pltpu.VMEM((384, KFIRST + KSECOND), bf16),
            pltpu.VMEM((3, 1536, 256), bf16),
            pltpu.VMEM((KFIRST, cz // CHUNKS), bf16),
            pltpu.VMEM((KSECOND, cz // CHUNKS), bf16),
            pltpu.VMEM((384, cz + 128), f32),
            pltpu.VMEM((64 * WINDOWS, 8, 128), f32),
            pltpu.VMEM((tiles, cap, 128), f32),
            pltpu.VMEM((tiles, cap), i32),
            pltpu.SMEM((tiles, cap), i32),
            pltpu.VMEM((tiles, 8, cap), f32),
            pltpu.VMEM((tiles, 8, cap), f32),
            pltpu.VMEM((tiles, cap), i32),
            dma((3,)),
            dma((5,)),
            pltpu.SemaphoreType.REGULAR,
            dma,
            dma,
            dma((2, CHUNKS)),
            dma((2, CHUNKS)),
            dma((2, CHUNKS)),
            dma((2, CHUNKS)),
            dma((2, CHUNKS)),
            dma((2, CHUNKS)),
            dma,
            dma,
        ],
        compiler_params=pltpu.CompilerParams(
            collective_id=0, has_side_effects=True, vmem_limit_bytes=60 * 1024 * 1024
        ),
        name="tidal",
    )(
        potential,
        gal_cells.reshape(tiles, cap),
        gal_z.reshape(tiles, cap),
        gal_bins.reshape(tiles, cap),
        gal_counts.reshape(1, tiles),
        jnp.asarray(plane_weights()),
        jnp.asarray(band_weights()),
    )
    return returned.reshape(6, 1, 1, tiles * cap)


def solution(mesh):
    return jax.shard_map(
        functools.partial(body, mesh.shape["gx"], mesh.shape["yz"]),
        mesh=mesh,
        in_specs=(
            P("gx", "yz", None),
            P("gx", "yz", None, None),
            P("gx", "yz", None, None),
            P("gx", "yz", None, None),
            P("gx", "yz", None),
        ),
        out_specs=P(None, "gx", "yz", None),
        check_vma=False,
    )
```

```python
import functools

import jax
import jax.numpy as jnp
import ml_dtypes
import numpy as np
from jax import lax
from jax.experimental import pallas as pl
from jax.experimental.pallas import tpu as pltpu
from jax.sharding import PartitionSpec as P

HALO = 6
BINS = 8
SIGMA = HALO / 3.0
STEP = 116
MESH = pl.DeviceIdType.MESH
CHUNKS = 4
PLANE = 8
STRIDE = 1
WINDOWS = 19
FIRST = 256
SECOND = 160
KROWS = FIRST + SECOND
KFIRST, KSECOND = 6 * FIRST, 1024
PARTS = (0, 1, 2, 0, 1, 0)
WEIGHT_PARTS = (0, 0, 0, 1, 1, 2)
ORDER = (0, 1, 5, 2, 3, 4)
GROUPS = ((0, 192, 0), (192, 320, 1), (320, 384, 2))


def filters():
    k = np.arange(-HALO, HALO + 1).astype(np.float64)
    w0 = np.exp(-k * k / (2.0 * SIGMA * SIGMA))
    w0 = w0 / w0.sum()
    return w0, k / SIGMA**2 * w0, (k * k / SIGMA**4 - 1.0 / SIGMA**2) * w0


def split3(a):
    parts = []
    for _ in range(3):
        p = a.astype(ml_dtypes.bfloat16)
        parts.append(p)
        a = a - p.astype(np.float64)
    return parts


def plane_weights():
    w = filters()
    rows = [(x, y) for x in range(8) for y in range(8)]
    rows += [(x, y) for x in range(-6, 0) for y in range(8)]
    rows += [(x, y) for x in range(8, 14) for y in range(8)]
    rows += [(x, y) for x in range(8) for y in range(-6, 0)]
    rows += [(x, y) for x in range(8) for y in range(8, 14)]
    outer = list(range(-6, 0)) + list(range(8, 14))
    for ys in (range(-6, 0), range(8, 14)):
        rows += [(x, y) for x in outer for y in ys] + [None] * 8
    pairs = ((2, 0), (0, 2), (1, 1), (1, 0), (0, 1), (0, 0))
    a = np.zeros((6, 8, 8, KROWS))
    for k, at in enumerate(rows):
        if at is None:
            continue
        for xo in range(8):
            dx = at[0] - xo + HALO
            for yo in range(8):
                dy = at[1] - yo + HALO
                if 0 <= dx <= 2 * HALO and 0 <= dy <= 2 * HALO:
                    for c, (fx, fy) in enumerate(pairs):
                        a[c, xo, yo, k] = w[fx][dx] * w[fy][dy]
    parts = split3(a.reshape(384, KROWS))
    out = np.zeros((384, KFIRST + KSECOND), ml_dtypes.bfloat16)
    for i, p in enumerate(WEIGHT_PARTS):
        out[:, i * FIRST : (i + 1) * FIRST] = parts[p][:, :FIRST]
        at = KFIRST + i * SECOND
        out[:, at : at + SECOND] = parts[p][:, FIRST:]
    return out


def band_weights():
    w = filters()
    out = np.zeros((3, 6 * 256, 256), ml_dtypes.bfloat16)
    for f in range(3):
        band = np.zeros((256, 256))
        for half in range(2):
            for lane in range(128):
                for tap in range(2 * HALO + 1):
                    band[half * STEP + lane + tap, half * 128 + lane] = w[f][tap]
        parts = split3(band)
        for i, p in enumerate(WEIGHT_PARTS):
            out[f, i * 256 : (i + 1) * 256] = parts[p]
    return out


def kernel(
    n_gx, n_yz, pot_hbm, cells_hbm, zeds_hbm, bins_hbm, counts_hbm, plane_hbm, band_hbm, out,
    pot, cells, zeds, bins, counts, msg, slots, xb, xa, up, down, cup, cdown, yb, ya, cb, ca,
    plane_w, band_w, first_in, second_in, partial, tab, wrow, addr_v, addr_s, served, returned, live,
    local_sem, in_sem, ready, slot_send, slot_recv, x_send, x_recv, y_send, y_recv, c_send, c_recv, ret_send, ret_recv,
):
    g = lax.axis_index("gx")
    t = lax.axis_index("yz")
    zc = pot.shape[2] // CHUNKS
    g_up, g_down = lax.rem(g + 1, n_gx), lax.rem(g + n_gx - 1, n_gx)
    t_up, t_down = lax.rem(t + 1, n_yz), lax.rem(t + n_yz - 1, n_yz)

    barrier = pltpu.get_barrier_semaphore()

    z, q = t // PLANE, lax.rem(t, PLANE)
    lines = n_yz // PLANE
    in_plane = [(g, z * PLANE + lax.rem(q + i, PLANE)) for i in range(1, PLANE)]
    in_line = [(g, lax.rem(z + i, lines) * PLANE + q) for i in range(1, lines)]
    for to in [(g_up, t), (g_down, t)] + in_plane + in_line:
        pl.semaphore_signal(barrier, inc=1, device_id=to, device_id_type=MESH)

    @pl.when(q == PLANE - 1)
    def _():
        pl.semaphore_signal(barrier, inc=1, device_id=(g, t_up), device_id_type=MESH)

    @pl.when(q == 0)
    def _():
        pl.semaphore_signal(barrier, inc=1, device_id=(g, t_down), device_id_type=MESH)

    loads = [
        pltpu.make_async_copy(src, dst, in_sem.at[i])
        for i, (src, dst) in enumerate(
            ((pot_hbm, pot), (cells_hbm, cells), (zeds_hbm, zeds), (bins_hbm, bins), (counts_hbm, counts))
        )
    ]
    for load in loads:
        load.start()
    plane_in = pltpu.make_async_copy(plane_hbm, plane_w, local_sem.at[0])
    band_in = pltpu.make_async_copy(band_hbm, band_w, local_sem.at[1])
    plane_in.start()
    band_in.start()
    for load in loads:
        load.wait()
    for i, ref in enumerate((cells, zeds, bins)):
        msg[:, i, :] = ref[...]
    for p in range(8):
        up[6 * p : 6 * p + 6, :] = pot[p, 2:8, :]
        down[6 * p : 6 * p + 6, :] = pot[p, 0:6, :]
    edge = jnp.logical_or(q == PLANE - 1, q == 0)

    @pl.when(edge)
    def _():
        pl.semaphore_wait(barrier, PLANE + lines + 1)

    @pl.when(jnp.logical_not(edge))
    def _():
        pl.semaphore_wait(barrier, PLANE + lines)

    def remote(src, dst, send, recv, to):
        return pltpu.make_async_remote_copy(
            src_ref=src, dst_ref=dst, send_sem=send, recv_sem=recv, device_id=to, device_id_type=MESH
        )

    x_copies, y_copies, c_copies = [], [], []
    for c in range(CHUNKS):
        zs = pl.ds(c * zc, zc)
        x_copies.append((
            remote(pot.at[pl.ds(2, 6), :, zs], xb.at[:, :, zs], x_send.at[0, c], x_recv.at[0, c], (g_up, t)),
            remote(pot.at[pl.ds(0, 6), :, zs], xa.at[:, :, zs], x_send.at[1, c], x_recv.at[1, c], (g_down, t)),
        ))
        y_copies.append((
            remote(up.at[:, zs], yb.at[:, zs], y_send.at[0, c], y_recv.at[0, c], (g, t_up)),
            remote(down.at[:, zs], ya.at[:, zs], y_send.at[1, c], y_recv.at[1, c], (g, t_down)),
        ))
        c_copies.append((
            remote(cup.at[:, zs], cb.at[:, zs], c_send.at[0, c], c_recv.at[0, c], (g, t_up)),
            remote(cdown.at[:, zs], ca.at[:, zs], c_send.at[1, c], c_recv.at[1, c], (g, t_down)),
        ))
    for copy in x_copies[0]:
        copy.start()
    for c in range(CHUNKS):
        for copy in y_copies[c]:
            copy.start()
    for copy in x_copies[0]:
        copy.wait_send()
    for copy in x_copies[1] + x_copies[2] + x_copies[3]:
        copy.start()
    for to in in_plane:
        pl.semaphore_signal(ready, inc=1, device_id=to, device_id_type=MESH)
    pl.semaphore_wait(ready, PLANE - 1)

    @pl.loop(1, n_yz)
    def _(i):
        to = lax.rem(t + i * STRIDE, n_yz)
        remote(msg.at[to], slots.at[t], slot_send, slot_recv, (g, to)).start()

    pltpu.make_async_copy(msg.at[t], slots.at[t], slot_recv).start()

    def corners(c):
        zs = pl.ds(c * zc, zc)
        for copy in x_copies[c]:
            copy.wait_recv()
        for side, ref, live in ((0, xb, g > 0), (1, xa, g < n_gx - 1)):
            @pl.when(jnp.logical_not(live))
            def _():
                ref[:, :, zs] = jnp.zeros((6, 8, zc), jnp.float32)

            for q in range(6):
                at = 36 * side + 6 * q
                cup[at : at + 6, zs] = ref[q, 2:8, zs]
                cdown[at : at + 6, zs] = ref[q, 0:6, zs]
        for copy in c_copies[c]:
            copy.start()

    def split(x):
        p1 = x.astype(jnp.bfloat16)
        r = x - p1.astype(jnp.float32)
        p2 = r.astype(jnp.bfloat16)
        return p1, p2, (r - p2.astype(jnp.float32)).astype(jnp.bfloat16)

    def place(ref, size, at, x):
        rows = x.shape[0]
        parts = split(x)
        for i, p in enumerate(PARTS):
            ref[i * size + at : i * size + at + rows, :] = parts[p]

    def first_part(c):
        zs = pl.ds(c * zc, zc)
        place(first_in, FIRST, 0, pot[:, :, zs].reshape(64, zc))
        place(first_in, FIRST, 64, xb[:, :, zs].reshape(48, zc))
        place(first_in, FIRST, 112, xa[:, :, zs].reshape(48, zc))
        for copy in y_copies[c]:
            copy.wait_recv()
        place(first_in, FIRST, 160, jnp.where(t > 0, yb[:, zs], 0.0))
        place(first_in, FIRST, 208, jnp.where(t < n_yz - 1, ya[:, zs], 0.0))
        partial[:, zs] = jnp.dot(plane_w[:, :KFIRST], first_in[...], preferred_element_type=jnp.float32)

    second_in[6 * SECOND :, :] = jnp.zeros((KSECOND - 6 * SECOND, zc), jnp.bfloat16)
    plane_in.wait()
    band_in.wait()
    for c in range(CHUNKS - 1):
        corners(c)
        first_part(c)

    pltpu.make_async_copy(msg, slots, slot_recv).wait()
    zr = jnp.bitwise_and(slots[:, 1, :] - HALO, 2047)
    window = jnp.right_shift(zr * 565, 16)
    addr_v[...] = slots[:, 0, :] * WINDOWS + window
    to_scalar = pltpu.make_async_copy(addr_v, addr_s, local_sem.at[2])
    to_scalar.start()
    zl = (zr - window * STEP).astype(jnp.float32)
    weight = (slots[:, 2, :].astype(jnp.float32) + 0.5) / BINS
    lane = lax.broadcasted_iota(jnp.int32, (128, 128), 1).astype(jnp.float32)
    columns = jnp.transpose(jnp.concatenate([zl, weight], axis=0))

    def interpolation_rows(homes):
        scale = SIGMA * SIGMA
        for h in homes:
            z_at = columns[:, h : h + 1]
            w_at = columns[:, 64 + h : 65 + h] * scale
            wrow[h] = jnp.where(lane == z_at, scale - w_at, jnp.where(lane == z_at + 1.0, w_at, 0.0))

    interpolation_rows(range(n_yz // 2))
    corners(3)
    first_part(3)
    flat = tab.reshape(64 * WINDOWS * 8, 128)

    def windows(lo, hi):
        parts = [split(partial[:, 2 * STEP * w : 2 * STEP * w + 256]) for w in range(lo, hi)]
        for a, b, f in GROUPS:
            lhs = jnp.concatenate([jnp.concatenate([g[p][a:b] for p in PARTS], axis=1) for g in parts], axis=0)
            h = jnp.dot(lhs, band_w[f], preferred_element_type=jnp.float32)
            at = 0
            for w in range(lo, hi):
                for comp in range(a // 64, b // 64):
                    for ct in range(8):
                        for half in range(2):
                            v = h[at : at + 8, 128 * half : 128 * half + 128]
                            first = ((8 * ct) * WINDOWS + 2 * w + half) * 8 + comp
                            flat[pl.ds(first, 8, stride=8 * WINDOWS), :] = v
                        at += 8

    def dense(c):
        zs = pl.ds(c * zc, zc)
        for copy in c_copies[c]:
            copy.wait_recv()
        first, last = t > 0, t < n_yz - 1
        zero8 = jnp.zeros((8, zc), jnp.float32)
        place(second_in, SECOND, 0, jnp.concatenate([jnp.where(first, cb[:, zs], 0.0), zero8], axis=0))
        place(second_in, SECOND, 80, jnp.concatenate([jnp.where(last, ca[:, zs], 0.0), zero8], axis=0))
        field = partial[:, zs] + jnp.dot(plane_w[:, KFIRST:], second_in[...], preferred_element_type=jnp.float32)
        partial[:, zs] = field
        if c == 0:
            partial[:, 2048:2176] = field[:, 0:128]
        lo, hi = 2 * c, 2 * c + (2 if c < CHUNKS - 1 else 3)
        windows(lo, hi)

    live[...] = jnp.transpose(jnp.broadcast_to(counts[...], (128, n_yz)))
    for c in range(CHUNKS - 1):
        dense(c)
    interpolation_rows(range(n_yz // 2, n_yz))
    dense(CHUNKS - 1)
    to_scalar.wait()
    lane8 = lax.broadcasted_iota(jnp.int32, (8, 128), 1)

    six = pl.ds(0, 6)

    def serve(h):
        acc = jnp.zeros((8, 128), jnp.float32)
        for j in range(128):
            row = addr_s[h, j]
            p = tab[row] * wrow[h, pl.ds(j, 1), :]
            acc = jnp.where(lane8 == j, jnp.sum(p, axis=1, keepdims=True), acc)
        served[h] = acc

    def serve_line(i, count):
        away = lines // 2 + (i + 1) // 2 * (1 - 2 * lax.rem(i, 2))
        homes = [lax.rem(z + away, lines) * PLANE + lax.rem(q + 1 + k, PLANE) for k in range(PLANE)]
        for h in homes:
            serve(h)
        for h in homes[:count]:
            remote(served.at[h, six], returned.at[t, six], ret_send, ret_recv, (g, h)).start()

    @pl.loop(0, lines - 1)
    def _(i):
        serve_line(i, PLANE)

    serve_line(lines - 1, PLANE - 1)
    pltpu.make_async_copy(served.at[t, six], returned.at[t, six], ret_recv).start()

    pltpu.make_async_copy(served.at[:, six], returned.at[:, six], ret_recv).wait()
    keep = lax.broadcasted_iota(jnp.int32, (n_yz, 128), 1) < live[...]
    for a, at in enumerate(ORDER):
        out[a] = jnp.where(keep, returned[:, at, :], 0.0)
    others = pl.ds(0, n_yz - 1)
    pltpu.make_async_copy(served.at[others, six], returned.at[others, six], ret_send).wait()
    pltpu.make_async_copy(msg.at[pl.ds(0, n_yz - 1)], slots.at[pl.ds(0, n_yz - 1)], slot_send).wait()
    for c in range(CHUNKS):
        for copy in (x_copies[c] if c else ()) + y_copies[c] + c_copies[c]:
            copy.wait_send()


def body(n_gx, n_yz, potential, gal_cells, gal_z, gal_bins, gal_counts):
    tiles, cap = gal_cells.shape[2], gal_cells.shape[3]
    cz = potential.shape[2]
    f32, bf16, i32 = jnp.float32, jnp.bfloat16, jnp.int32
    vmem = pl.BlockSpec(memory_space=pltpu.VMEM)
    hbm = pl.BlockSpec(memory_space=pl.ANY)
    dma = pltpu.SemaphoreType.DMA
    returned = pl.pallas_call(
        functools.partial(kernel, n_gx, n_yz),
        out_shape=jax.ShapeDtypeStruct((6, tiles, cap), f32),
        in_specs=[hbm] * 7,
        out_specs=vmem,
        scratch_shapes=[
            pltpu.VMEM(potential.shape, f32),
            pltpu.VMEM((tiles, cap), i32),
            pltpu.VMEM((tiles, cap), i32),
            pltpu.VMEM((tiles, cap), i32),
            pltpu.VMEM((1, tiles), i32),
            pltpu.VMEM((tiles, 4, cap), i32),
            pltpu.VMEM((tiles, 4, cap), i32),
            pltpu.VMEM((6, 8, cz), f32),
            pltpu.VMEM((6, 8, cz), f32),
            pltpu.VMEM((48, cz), f32),
            pltpu.VMEM((48, cz), f32),
            pltpu.VMEM((72, cz), f32),
            pltpu.VMEM((72, cz), f32),
            pltpu.VMEM((48, cz), f32),
            pltpu.VMEM((48, cz), f32),
            pltpu.VMEM((72, cz), f32),
            pltpu.VMEM((72, cz), f32),
            pltpu.VMEM((384, KFIRST + KSECOND), bf16),
            pltpu.VMEM((3, 1536, 256), bf16),
            pltpu.VMEM((KFIRST, cz // CHUNKS), bf16),
            pltpu.VMEM((KSECOND, cz // CHUNKS), bf16),
            pltpu.VMEM((384, cz + 128), f32),
            pltpu.VMEM((64 * WINDOWS, 8, 128), f32),
            pltpu.VMEM((tiles, cap, 128), f32),
            pltpu.VMEM((tiles, cap), i32),
            pltpu.SMEM((tiles, cap), i32),
            pltpu.VMEM((tiles, 8, cap), f32),
            pltpu.VMEM((tiles, 8, cap), f32),
            pltpu.VMEM((tiles, cap), i32),
            dma((3,)),
            dma((5,)),
            pltpu.SemaphoreType.REGULAR,
            dma,
            dma,
            dma((2, CHUNKS)),
            dma((2, CHUNKS)),
            dma((2, CHUNKS)),
            dma((2, CHUNKS)),
            dma((2, CHUNKS)),
            dma((2, CHUNKS)),
            dma,
            dma,
        ],
        compiler_params=pltpu.CompilerParams(
            collective_id=0, has_side_effects=True, vmem_limit_bytes=60 * 1024 * 1024
        ),
        name="tidal",
    )(
        potential,
        gal_cells.reshape(tiles, cap),
        gal_z.reshape(tiles, cap),
        gal_bins.reshape(tiles, cap),
        gal_counts.reshape(1, tiles),
        jnp.asarray(plane_weights()),
        jnp.asarray(band_weights()),
    )
    return returned.reshape(6, 1, 1, tiles * cap)


def solution(mesh):
    return jax.shard_map(
        functools.partial(body, mesh.shape["gx"], mesh.shape["yz"]),
        mesh=mesh,
        in_specs=(
            P("gx", "yz", None),
            P("gx", "yz", None, None),
            P("gx", "yz", None, None),
            P("gx", "yz", None, None),
            P("gx", "yz", None),
        ),
        out_specs=P(None, "gx", "yz", None),
        check_vma=False,
    )
```
